512 devices in a mesh: dp: 16 (over y, core), cuts: 32 (over x, z).
Axes of the slice: x: 4, y: 8, z: 8, core: 2. Of those that a mesh axis runs over, the one named last changes fastest.
Arguments:
- tokens: bfloat16 [1024, 6144], P('cuts', 'dp'), may hold values from -6 to 6
- cotangent: bfloat16 [1024, 6144], P('cuts', 'dp'), may hold values from -6 to 6
- w_gate: bfloat16 [2, 6144, 16384], P(None, 'dp', 'cuts'), may hold values from -0.078125 to 0.078125
- w_up: bfloat16 [2, 6144, 16384], P(None, 'dp', 'cuts'), may hold values from -0.078125 to 0.078125
- w_down: bfloat16 [2, 16384, 6144], P(None, 'cuts', 'dp'), may hold values from -0.046875 to 0.046875
- row_token: int32 [1024], replicated, may hold values from 0 to 1023, each once
- block_expert: int32 [8, 1], replicated, may hold values from 0 to 1; in each aligned block of 8 rows (0 to 7, 8 to 15, ...) at most 6 rows name the same one
- gate_weight: float32 [1024], replicated, may hold values from 0.1 to 1
Outputs:
- token_grad: bfloat16 [1024, 6144], P('cuts', 'dp')
- grad_gate: bfloat16 [2, 6144, 16384], P(None, 'dp', 'cuts')
- grad_up: bfloat16 [2, 6144, 16384], P(None, 'dp', 'cuts')
- grad_down: bfloat16 [2, 16384, 6144], P(None, 'cuts', 'dp')
The draws below stay inside these ranges and needn't reach their ends.
Inputs may be any that keep to these rules, and one draw needn't show every extreme that they name: `row_token`: each token is held by exactly one row. `block_expert`: no expert serves more than 6 blocks, and one serves exactly 6.
All inputs are finite; a program needn't handle non-finite values.
Results may differ from the reference program's by a relative error of at most 0.0057.
Values may be sent and summed in bfloat16 or wider, within the bound.
No kernel may reach another device: no remote copies, remote signals or barrier semaphores. Data moves between devices by JAX's collectives and lax.ppermute only.
A program may use at most 64 MiB of HBM per device.

```python
import math
import jax
import jax.numpy as jnp
import numpy as np
from jax import lax

D = 6144
FF = 16384
E = 2
BLK = 128
NTOK = 1024
NB = 8
CAP = 6
N_DP = 16
N_CUTS = 32


def block_scale(own_key, dims, cuts, least, largest):
    factor_of = 1.0
    for dim, blocks in cuts:
        heights = jax.random.uniform(jax.random.fold_in(jax.random.fold_in(own_key, 6), dim), (blocks,), jnp.float32, least / len(cuts), largest / len(cuts))
        factor_of = factor_of * jnp.repeat(jnp.exp(heights), dims[dim] // blocks).reshape((-1,) + (1,) * (len(dims) - 1 - dim))
    return factor_of


def routed_block(stream_key, own, number, rows, count, top, limit, skew):
    order = jax.random.permutation(stream_key, count)
    packed, ordinary = load_shares(count, rows * top, limit, skew, True), load_shares(count, rows * top, limit, skew, False)
    places = jnp.arange(count)

    def named(tallies, rotation):
        used = int((tallies > 0).sum())
        fixed = max(1, used // 4)
        shifted = fixed + (places - fixed + rotation * (used - fixed)) % max(1, count - fixed)
        return jnp.zeros((count,), jnp.int32).at[order[jnp.where(places < fixed, places, shifted)]].set(jnp.asarray(tallies, jnp.int32))

    tallies = jnp.where(number % 4 == 0, named(packed, number // 4), named(ordinary, number - number // 4 - 1))
    mixed = jax.random.permutation(jax.random.fold_in(own, 3), count)
    source_of, sink = mixed[0:count // 2 * 2:2], mixed[1:count // 2 * 2:2]
    slack = jnp.minimum(tallies[source_of] - 1, limit - tallies[sink]) // 2
    slack = jnp.where((source_of == order[0]) | (sink == order[0]) | (tallies[sink] == 0), 0, jnp.maximum(slack, 0))
    shifted = jax.random.randint(jax.random.fold_in(own, 4), (count // 2,), 0, 1 << 20) % (slack + 1)
    tallies = tallies.at[source_of].add(-shifted).at[sink].add(shifted)
    members = jnp.searchsorted(jnp.cumsum(tallies), jnp.arange(rows * top), side="right").astype(jnp.int32)
    listing = members.reshape(top, rows).T
    listing = listing[jax.random.permutation(jax.random.fold_in(own, 1), rows)]
    rotation = jax.random.randint(jax.random.fold_in(own, 2), (rows, 1), 0, top)
    return jnp.take_along_axis(listing, (jnp.arange(top)[None, :] + rotation) % top, axis=1)


def load_shares(count, total, most, skew, full):
    loads = [(1 << 20) // math.isqrt(standing ** skew) + 1 for standing in range(1, count + 1)]
    largest = most if full else min(most, max(-(-total // count), total * loads[0] // sum(loads)))
    least = 1 if total - largest >= count - 1 else 0
    counts, surplus = [largest] + [least] * (count - 1), total - largest - least * (count - 1)
    while surplus > 0:
        free = [i for i in range(1, count) if counts[i] < largest] or [i for i in range(1, count) if counts[i] < most]
        whole, remaining = sum([loads[i] for i in free]), surplus
        for i in free:
            addition = min(most - counts[i], max(1, remaining * loads[i] // whole), surplus)
            counts[i] = counts[i] + addition
            surplus = surplus - addition
    return np.array(counts)


def gaussian(rng, dims, deviation, bound, cuts=(), kind=jnp.bfloat16):
    gain = block_scale(rng, dims, cuts, -0.22, 0.18) if cuts else 1.0
    array = jax.random.normal(rng, dims, jnp.float32) * deviation * gain
    return jnp.minimum(jnp.maximum(array, -bound), bound).astype(kind)


def setup_inputs(seed: int = 0) -> dict:
    keys = jax.random.split(jax.random.key(seed), 9)
    tokens = gaussian(keys[0], (NTOK, D), 1.0, 6.0, ((0, 32), (1, 16)))
    cotangent = gaussian(keys[1], (NTOK, D), 1.0, 6.0, ((0, 32), (1, 16)))
    w_gate = gaussian(keys[2], (E, D, FF), D ** -0.5, 0.078125, ((1, 16), (2, 32)))
    w_up = gaussian(keys[3], (E, D, FF), D ** -0.5, 0.078125, ((1, 16), (2, 32)))
    w_down = gaussian(keys[4], (E, FF, D), FF ** -0.5, 0.046875, ((1, 32), (2, 16)))
    row_token = jax.random.permutation(keys[5], NTOK).astype(jnp.int32)
    block_expert_keys = jax.random.split(jax.random.fold_in(keys[6], 1), NB // NB)
    block_expert_turns = jax.random.permutation(jax.random.fold_in(keys[6], 3), NB // NB)
    block_expert = jax.vmap(lambda own, number: routed_block(jax.random.fold_in(keys[6], 2), own, number, NB, E, 1, CAP, 2))(block_expert_keys, block_expert_turns).reshape((NB, 1))
    gate_weight = jnp.clip(jnp.exp(jax.random.uniform(keys[7], (NTOK,), jnp.float32, math.log(0.1), math.log(1.0))), 0.1, 1.0)
    return dict(tokens=tokens, cotangent=cotangent, w_gate=w_gate, w_up=w_up, w_down=w_down, row_token=row_token, block_expert=block_expert, gate_weight=gate_weight)


def split_sum(partials):
    return jnp.sum(partials, axis=0)


def activate(gate_pre, up_pre, down_grad):
    sigmoid_val = jax.nn.sigmoid(gate_pre)
    swish_val = gate_pre * sigmoid_val
    hidden = (swish_val * up_pre).astype(jnp.bfloat16)
    slope_val = sigmoid_val * (1.0 + gate_pre * (1.0 - sigmoid_val))
    gate_grad = (down_grad * up_pre * slope_val).astype(jnp.bfloat16)
    up_grad = (down_grad * swish_val).astype(jnp.bfloat16)
    return hidden, gate_grad, up_grad


def reference(tokens, cotangent, w_gate, w_up, w_down, row_token, block_expert, gate_weight):
    token_rows = tokens[row_token]
    cot_rows = (cotangent[row_token].astype(jnp.float32) * gate_weight[:, None]).astype(jnp.bfloat16)
    expert_ids = block_expert[:, 0].astype(jnp.int32)
    slice_dp = D // N_DP
    slice_cut = FF // N_CUTS

    def block_pass(block_args):
        tok_block, cot_block, expert = block_args
        gate_mat = lax.dynamic_index_in_dim(w_gate, expert, 0, False).astype(jnp.float32)
        up_mat = lax.dynamic_index_in_dim(w_up, expert, 0, False).astype(jnp.float32)
        down_mat = lax.dynamic_index_in_dim(w_down, expert, 0, False).astype(jnp.float32)
        tok_split = tok_block.astype(jnp.float32).reshape(BLK, N_DP, slice_dp)
        cot_split = cot_block.astype(jnp.float32).reshape(BLK, N_DP, slice_dp)
        gate_pre = split_sum(jnp.einsum('bjd,jdf->jbf', tok_split, gate_mat.reshape(N_DP, slice_dp, FF)))
        up_pre = split_sum(jnp.einsum('bjd,jdf->jbf', tok_split, up_mat.reshape(N_DP, slice_dp, FF)))
        down_grad = split_sum(jnp.einsum('bjd,fjd->jbf', cot_split, down_mat.reshape(FF, N_DP, slice_dp)))
        hidden, gate_grad, up_grad = activate(gate_pre, up_pre, down_grad)
        gg_split = gate_grad.astype(jnp.float32).reshape(BLK, N_CUTS, slice_cut)
        ug_split = up_grad.astype(jnp.float32).reshape(BLK, N_CUTS, slice_cut)
        terms = jnp.einsum('bcf,dcf->cbd', gg_split, gate_mat.reshape(D, N_CUTS, slice_cut))
        terms = terms + jnp.einsum('bcf,dcf->cbd', ug_split, up_mat.reshape(D, N_CUTS, slice_cut))
        return hidden, gate_grad, up_grad, split_sum(terms)

    tok_blocks = token_rows.reshape(NB, BLK, D)
    cot_blocks = cot_rows.reshape(NB, BLK, D)
    hidden, gate_grad, up_grad, row_grad = lax.map(block_pass, (tok_blocks, cot_blocks, expert_ids))
    hidden = hidden.reshape(NTOK, FF)
    gate_grad = gate_grad.reshape(NTOK, FF)
    up_grad = up_grad.reshape(NTOK, FF)
    row_grad = row_grad.reshape(NTOK, D)
    row_expert = jnp.repeat(expert_ids, BLK)

    def expert_grads(expert):
        row_mask = (row_expert == expert).astype(jnp.bfloat16)[:, None]
        grad_g = jnp.dot(token_rows.T, gate_grad * row_mask, preferred_element_type=jnp.float32)
        grad_u = jnp.dot(token_rows.T, up_grad * row_mask, preferred_element_type=jnp.float32)
        grad_d = jnp.dot((hidden * row_mask).T, cot_rows, preferred_element_type=jnp.float32)
        return grad_g.astype(jnp.bfloat16), grad_u.astype(jnp.bfloat16), grad_d.astype(jnp.bfloat16)

    grad_gate, grad_up, grad_down = lax.map(expert_grads, jnp.arange(E, dtype=jnp.int32))
    inverse = jnp.argsort(row_token).astype(jnp.int32)
    token_grad = row_grad[inverse].astype(jnp.bfloat16)
    return token_grad, grad_gate, grad_up, grad_down
```

```python
import functools

import jax
import jax.numpy as jnp
from jax import lax
from jax.experimental import pallas as pl
from jax.experimental.pallas import tpu as pltpu
from jax.sharding import Mesh
from jax.sharding import PartitionSpec as P

BF = jnp.bfloat16
F32 = jnp.float32
ROWS = 256
VMEM_BYTES = 48 * 2**20


def dot(a, b, ca, cb):
    return lax.dot_general(a, b, (((ca,), (cb,)), ((), ())), preferred_element_type=F32)


def activate(gate_pre, up_pre, down_grad):
    sigmoid_val = jax.nn.sigmoid(gate_pre)
    swish_val = gate_pre * sigmoid_val
    slope_val = sigmoid_val * (1.0 + gate_pre * (1.0 - sigmoid_val))
    gate_grad = (down_grad * up_pre * slope_val).astype(BF)
    up_grad = (down_grad * swish_val).astype(BF)
    return gate_grad, up_grad


def call(body, outs, flops, args):
    in_specs = [
        pl.BlockSpec(memory_space=pltpu.SMEM if a.ndim == 1 else pltpu.VMEM) for a in args
    ]
    moved = sum(a.size * a.dtype.itemsize for a in (*args, *outs))
    return pl.pallas_call(
        body,
        out_shape=outs,
        in_specs=in_specs,
        out_specs=[pl.BlockSpec(memory_space=pltpu.VMEM) for _ in outs],
        compiler_params=pltpu.CompilerParams(vmem_limit_bytes=VMEM_BYTES),
        cost_estimate=pl.CostEstimate(flops=flops, bytes_accessed=moved, transcendentals=0),
    )(*args)


def by_expert(rows, expert, experts):
    return [jnp.where(expert == e, rows, jnp.zeros_like(rows)) for e in range(experts)]


def forward_body(cb, n_w, core_ref, x_ref, expert_ref, *refs):
    w_refs, (keep_ref, give_ref) = refs[:n_w], refs[n_w:]
    n_y, part, width = keep_ref.shape
    experts = w_refs[0].shape[0]
    hid = width // n_w
    core = core_ref[0]
    pairs = ROWS // (2 * part)

    @pl.loop(0, n_y // pairs)
    def _(i):
        at = pl.ds(pl.multiple_of(i * ROWS, ROWS), ROWS)
        masked = by_expert(x_ref[at, :], expert_ref[at, :], experts)
        for k, w_ref in enumerate(w_refs):
            out = dot(masked[0], w_ref[0], 1, cb)
            for e in range(1, experts):
                out = out + dot(masked[e], w_ref[e], 1, cb)
            for j in range(pairs):
                lo = out[2 * j * part : (2 * j + 1) * part]
                hi = out[(2 * j + 1) * part : (2 * j + 2) * part]
                cols = slice(k * hid, (k + 1) * hid)
                keep_ref[i * pairs + j, :, cols] = jnp.where(core == 0, lo, hi)
                give_ref[i * pairs + j, :, cols] = jnp.where(core == 0, hi, lo).astype(BF)


def terms_body(x_ref, expert_ref, gate_ref, up_ref, out_ref):
    experts, _, hid = gate_ref.shape

    @pl.loop(0, x_ref.shape[0] // ROWS)
    def _(i):
        at = pl.ds(pl.multiple_of(i * ROWS, ROWS), ROWS)
        expert = expert_ref[at, :]
        gates = by_expert(x_ref[at, :hid], expert, experts)
        ups = by_expert(x_ref[at, hid:], expert, experts)
        out = 0.0
        for e in range(experts):
            out = out + dot(gates[e], gate_ref[e], 1, 1) + dot(ups[e], up_ref[e], 1, 1)
        out_ref[at, :] = out.astype(BF)


def total_body(x_ref, out_ref):
    out = x_ref[0].astype(F32)
    for i in range(1, x_ref.shape[0]):
        out = out + x_ref[i].astype(F32)
    out_ref[...] = out.astype(BF)


def make(n_y, n_core, n_x, n_z):
    dp, cuts = ("y", "core"), ("x", "z")
    n_dp, n_cuts = n_y * n_core, n_x * n_z
    swap = [(i, n_core - 1 - i) for i in range(n_core)]

    def per_device(tokens, cotangent, w_gate, w_up, w_down, row_token, block_expert, gate_weight):
        own, cols = tokens.shape
        n_tok = row_token.shape[0]
        experts, _, hid = w_gate.shape
        blk = n_tok // block_expert.shape[0]
        part = n_tok // n_dp
        core = lax.axis_index("core").astype(jnp.int32).reshape(1)
        first = (lax.axis_index("x") * n_z + lax.axis_index("z")) * own
        work = 2 * n_tok * experts * cols * hid

        expert_row = jnp.repeat(block_expert[:, 0], blk)
        holds = row_token[None, :] == jnp.arange(n_tok, dtype=jnp.int32)[:, None]
        expert_tok = jnp.sum(jnp.where(holds, expert_row[None, :], 0), axis=1)[:, None]
        holds_own = row_token[None, :] == first + jnp.arange(own, dtype=jnp.int32)[:, None]
        weight_own = jnp.sum(jnp.where(holds_own, gate_weight[None, :], 0.0), axis=1)
        cot_own = (cotangent.astype(F32) * weight_own[:, None]).astype(BF)

        def spread(rows):
            return jnp.broadcast_to(rows[None], (n_cuts,) + rows.shape)

        def exchange(x, axes):
            return lax.all_to_all(x, axes, split_axis=0, concat_axis=0, tiled=True)

        def reduce_dp(x, cb, weights):
            shape = (n_y, part, len(weights) * hid)
            outs = [jax.ShapeDtypeStruct(shape, F32), jax.ShapeDtypeStruct(shape, BF)]
            body = functools.partial(forward_body, cb, len(weights))
            keep, give = call(body, outs, work * len(weights), (core, x, expert_tok, *weights))
            came = lax.ppermute(give, "core", swap)
            chip = (keep + came.astype(F32)).astype(BF)
            return jnp.sum(exchange(chip, "y").astype(F32), axis=0)

        tok = exchange(spread(tokens), cuts)
        tok, cot_spread = lax.optimization_barrier((tok, spread(cot_own)))
        cot = exchange(cot_spread, cuts).reshape(n_tok, cols)
        tok = tok.reshape(n_tok, cols)

        pre = reduce_dp(tok, 0, (w_gate, w_up))
        gate_pre, up_pre = pre[:, :hid], pre[:, hid:]
        hidden = (gate_pre * jax.nn.sigmoid(gate_pre) * up_pre).astype(BF)
        gate_pre, up_pre, hidden = lax.optimization_barrier((gate_pre, up_pre, hidden))
        hidden = lax.all_gather(hidden, dp, axis=0, tiled=True)
        down_grad = reduce_dp(cot, 1, (w_down,))
        grads = jnp.concatenate(activate(gate_pre, up_pre, down_grad), axis=1)
        grads = lax.all_gather(grads, dp, axis=0, tiled=True)

        outs = [jax.ShapeDtypeStruct((n_tok, cols), BF)]
        (terms,) = call(terms_body, outs, 2 * work, (grads, expert_tok, w_gate, w_up))
        terms = exchange(terms.reshape(n_cuts, own, cols), cuts)
        outs = [jax.ShapeDtypeStruct((own, cols), BF)]
        (token_grad,) = call(total_body, outs, terms.size, (terms,))

        masks = [expert_tok == e for e in range(experts)]
        tok_by = jnp.concatenate([jnp.where(m, tok, 0) for m in masks], axis=1)
        grad_gate = dot(tok_by, grads[:, :hid], 0, 0).astype(BF).reshape(w_gate.shape)
        grad_up = dot(tok_by, grads[:, hid:], 0, 0).astype(BF).reshape(w_up.shape)
        grad_down = [dot(hidden, jnp.where(m, cot, 0), 0, 0).astype(BF) for m in masks]
        return token_grad, grad_gate, grad_up, jnp.stack(grad_down)

    return per_device


def solution(mesh):
    n_y, n_core, n_x, n_z = 8, 2, 4, 8
    fine = Mesh(mesh.devices.reshape(n_y, n_core, n_x, n_z), ("y", "core", "x", "z"))
    dp, cuts = ("y", "core"), ("x", "z")
    return jax.shard_map(
        make(n_y, n_core, n_x, n_z),
        mesh=fine,
        in_specs=(
            P(cuts, dp),
            P(cuts, dp),
            P(None, dp, cuts),
            P(None, dp, cuts),
            P(None, cuts, dp),
            P(),
            P(),
            P(),
        ),
        out_specs=(P(cuts, dp), P(None, dp, cuts), P(None, dp, cuts), P(None, cuts, dp)),
        check_vma=False,
    )
```

```python
import functools

import jax
import jax.numpy as jnp
from jax import lax
from jax.experimental import pallas as pl
from jax.experimental.pallas import tpu as pltpu
from jax.sharding import Mesh
from jax.sharding import PartitionSpec as P

BF = jnp.bfloat16
F32 = jnp.float32
ROWS = 256
VMEM_BYTES = 20 * 2**20


def dot(a, b, ca, cb):
    return lax.dot_general(a, b, (((ca,), (cb,)), ((), ())), preferred_element_type=F32)


def activate(gate_pre, up_pre, down_grad):
    sigmoid_val = jax.nn.sigmoid(gate_pre)
    swish_val = gate_pre * sigmoid_val
    hidden = (swish_val * up_pre).astype(BF)
    slope_val = sigmoid_val * (1.0 + gate_pre * (1.0 - sigmoid_val))
    gate_grad = (down_grad * up_pre * slope_val).astype(BF)
    up_grad = (down_grad * swish_val).astype(BF)
    return hidden, gate_grad, up_grad


def call(body, outs, flops, args):
    in_specs = [
        pl.BlockSpec(memory_space=pltpu.SMEM if a.ndim == 1 else pltpu.VMEM) for a in args
    ]
    moved = sum(a.size * a.dtype.itemsize for a in (*args, *outs))
    return pl.pallas_call(
        body,
        out_shape=outs,
        in_specs=in_specs,
        out_specs=[pl.BlockSpec(memory_space=pltpu.VMEM) for _ in outs],
        compiler_params=pltpu.CompilerParams(vmem_limit_bytes=VMEM_BYTES),
        cost_estimate=pl.CostEstimate(flops=flops, bytes_accessed=moved, transcendentals=0),
    )(*args)


def by_expert(rows, expert, experts):
    return [jnp.where(expert == e, rows, jnp.zeros_like(rows)) for e in range(experts)]


def forward_body(core_ref, expert_ref, wg_ref, wu_ref, wd_ref, *refs):
    chunks, (tok_ref, cot_ref, keep_ref, give_ref) = refs[:-4], refs[-4:]
    n_y, part, _ = keep_ref.shape
    experts, cols, hid = wg_ref.shape
    n_z = len(chunks) - 1
    step = tok_ref.shape[0] // n_z
    core = core_ref[0]
    pairs = ROWS // (2 * part)
    far = n_z // 2
    for i in range(n_z):
        at = slice(i * step, (i + 1) * step)
        if i == far:
            tok, cot = chunks[far][...], chunks[n_z][...]
        else:
            tok, cot = chunks[i][:, 0], chunks[i][:, 1]
        tok_ref[at, :] = tok.reshape(step, cols)
        cot_ref[at, :] = cot.reshape(step, cols)

    @pl.loop(0, n_y // pairs)
    def _(i):
        at = pl.ds(pl.multiple_of(i * ROWS, ROWS), ROWS)
        expert = expert_ref[at, :]
        toks = by_expert(tok_ref[at, :], expert, experts)
        cots = by_expert(cot_ref[at, :], expert, experts)
        for k, (xs, w_ref, cb) in enumerate(((toks, wg_ref, 0), (toks, wu_ref, 0), (cots, wd_ref, 1))):
            out = dot(xs[0], w_ref[0], 1, cb)
            for e in range(1, experts):
                out = out + dot(xs[e], w_ref[e], 1, cb)
            for j in range(pairs):
                lo = out[2 * j * part : (2 * j + 1) * part]
                hi = out[(2 * j + 1) * part : (2 * j + 2) * part]
                to = slice(k * hid, (k + 1) * hid)
                keep_ref[i * pairs + j, :, to] = jnp.where(core == 0, lo, hi)
                give_ref[i * pairs + j, :, to] = jnp.where(core == 0, hi, lo).astype(BF)


def terms_body(at_ref, expert_ref, gate_ref, up_ref, own_ref, other_ref, grads_ref, out_ref):
    experts, _, hid = gate_ref.shape
    n_y, n_core, part, width = grads_ref.shape
    n_x, n_z, own, cols = out_ref.shape
    y, core, z = at_ref[0], at_ref[1], at_ref[2]
    for i in range(n_y):
        to = lax.rem(y + i, n_y)
        grads_ref[to, core] = own_ref[i]
        grads_ref[to, 1 - core] = other_ref[i]
    per_y = n_core * part
    per_z = n_x * own

    @pl.loop(0, n_y * per_y // ROWS)
    def _(i):
        at = pl.ds(pl.multiple_of(i * ROWS, ROWS), ROWS)
        expert = expert_ref[at, :]
        rows = grads_ref[pl.ds(i * (ROWS // per_y), ROWS // per_y)].reshape(ROWS, width)
        gates = by_expert(rows[:, :hid], expert, experts)
        ups = by_expert(rows[:, hid:], expert, experts)
        out = 0.0
        for e in range(experts):
            out = out + dot(gates[e], gate_ref[e], 1, 1) + dot(ups[e], up_ref[e], 1, 1)
        out = out.astype(BF)
        for j in range(ROWS // per_z):
            to = lax.rem(z + i * (ROWS // per_z) + j, n_z)
            for x in range(n_x):
                out_ref[x, to] = out[j * per_z + x * own : j * per_z + (x + 1) * own]


def total_body(x_ref, out_ref):
    out = x_ref[0].astype(F32)
    for i in range(1, x_ref.shape[0]):
        out = out + x_ref[i].astype(F32)
    out_ref[...] = out.astype(BF)


def ring(x, axis, n, first, second):
    up = [(i, (i + 1) % n) for i in range(n)]
    down = [(i, (i - 1) % n) for i in range(n)]
    got = [x] + [None] * (n - 1)
    a = b = x
    for s in range(1, n // 2):
        a, b = lax.ppermute(a, axis, up), lax.ppermute(b, axis, down)
        got[n - s], got[s] = a, b
    got[n // 2] = (lax.ppermute(first(a), axis, up), lax.ppermute(second(b), axis, down))
    return got


def make(n_y, n_core, n_x, n_z):
    dp, cuts = ("y", "core"), ("x", "z")
    n_dp, n_cuts = n_y * n_core, n_x * n_z
    swap = [(i, n_core - 1 - i) for i in range(n_core)]

    def per_device(tokens, cotangent, w_gate, w_up, w_down, row_token, block_expert, gate_weight):
        own, cols = tokens.shape
        n_tok = row_token.shape[0]
        experts, _, hid = w_gate.shape
        blk = n_tok // block_expert.shape[0]
        part = n_tok // n_dp
        place = [lax.axis_index(a).astype(jnp.int32) for a in ("y", "core", "x", "z")]
        y, core, x, z = place
        work = 2 * n_tok * experts * cols * hid

        def exchange(v, axes):
            return lax.all_to_all(v, axes, split_axis=0, concat_axis=0, tiled=True)

        first = (x * n_z + z) * own
        holds_own = row_token[None, :] == first + jnp.arange(own, dtype=jnp.int32)[:, None]
        weight_own = jnp.sum(jnp.where(holds_own, gate_weight[None, :], 0.0), axis=1)
        cot_own = (cotangent.astype(F32) * weight_own[:, None]).astype(BF)
        both = jnp.stack([tokens, cot_own])
        both = exchange(jnp.broadcast_to(both[None], (n_x,) + both.shape), "x")
        chunks = ring(both, "z", n_z, lambda v: v[:, 0], lambda v: v[:, 1])
        far = chunks[n_z // 2]
        chunks[n_z // 2] = far[0]
        chunks.append(far[1])

        from_z = lax.rem(z + jnp.arange(n_z, dtype=jnp.int32), n_z)[:, None, None]
        from_x = jnp.arange(n_x, dtype=jnp.int32)[None, :, None]
        row_id = (from_x * n_z + from_z) * own + jnp.arange(own, dtype=jnp.int32)[None, None, :]
        row_id = row_id.reshape(n_tok)
        expert_row = jnp.repeat(block_expert[:, 0], blk)
        holds = row_token[None, :] == row_id[:, None]
        expert_tok = jnp.sum(jnp.where(holds, expert_row[None, :], 0), axis=1)[:, None]

        outs = [
            jax.ShapeDtypeStruct((n_tok, cols), BF),
            jax.ShapeDtypeStruct((n_tok, cols), BF),
            jax.ShapeDtypeStruct((n_y, part, 3 * hid), F32),
            jax.ShapeDtypeStruct((n_y, part, 3 * hid), BF),
        ]
        args = (core.reshape(1), expert_tok, w_gate, w_up, w_down, *chunks)
        tok, cot, keep, give = call(forward_body, outs, 3 * work, args)
        came = lax.ppermute(give, "core", swap)
        chip = (keep + came.astype(F32)).astype(BF)
        pre = jnp.sum(exchange(chip, "y").astype(F32), axis=0)
        hidden, gate_grad, up_grad = activate(
            pre[:, :hid], pre[:, hid : 2 * hid], pre[:, 2 * hid :]
        )
        hidden = lax.all_gather(hidden, dp, axis=0, tiled=True)
        grads = jnp.concatenate([gate_grad, up_grad], axis=1)
        parts = ring(grads, "y", n_y, lambda v: v[:, :hid], lambda v: v[:, hid:])
        parts[n_y // 2] = jnp.concatenate(parts[n_y // 2], axis=1)
        mine = jnp.stack(parts)
        others = lax.ppermute(mine, "core", swap)

        outs = [
            jax.ShapeDtypeStruct((n_y, n_core, part, 2 * hid), BF),
            jax.ShapeDtypeStruct((n_x, n_z, own, cols), BF),
        ]
        args = (jnp.stack([y, core, z]), expert_tok, w_gate, w_up, mine, others)
        grads, terms = call(terms_body, outs, 2 * work, args)
        grads, hidden = lax.optimization_barrier((grads.reshape(n_tok, 2 * hid), hidden))
        terms = exchange(terms.reshape(n_cuts, own, cols), cuts)
        outs = [jax.ShapeDtypeStruct((own, cols), BF)]
        (token_grad,) = call(total_body, outs, terms.size, (terms,))

        masks = [expert_tok == e for e in range(experts)]
        tok_by = jnp.concatenate([jnp.where(m, tok, 0) for m in masks], axis=1)
        grad_gate = dot(tok_by, grads[:, :hid], 0, 0).astype(BF).reshape(w_gate.shape)
        grad_up = dot(tok_by, grads[:, hid:], 0, 0).astype(BF).reshape(w_up.shape)
        grad_down = [dot(hidden, jnp.where(m, cot, 0), 0, 0).astype(BF) for m in masks]
        return token_grad, grad_gate, grad_up, jnp.stack(grad_down)

    return per_device


def solution(mesh):
    n_y, n_core, n_x, n_z = 8, 2, 4, 8
    fine = Mesh(mesh.devices.reshape(n_y, n_core, n_x, n_z), ("y", "core", "x", "z"))
    dp, cuts = ("y", "core"), ("x", "z")
    return jax.shard_map(
        make(n_y, n_core, n_x, n_z),
        mesh=fine,
        in_specs=(
            P(cuts, dp),
            P(cuts, dp),
            P(None, dp, cuts),
            P(None, dp, cuts),
            P(None, cuts, dp),
            P(),
            P(),
            P(),
        ),
        out_specs=(P(cuts, dp), P(None, dp, cuts), P(None, dp, cuts), P(None, cuts, dp)),
        check_vma=False,
    )
```

```python
import functools

import jax
import jax.numpy as jnp
from jax import lax
from jax.experimental import pallas as pl
from jax.experimental.pallas import tpu as pltpu
from jax.sharding import Mesh
from jax.sharding import PartitionSpec as P

BF = jnp.bfloat16
F32 = jnp.float32
ROWS = 256
CUT = 256
VMEM_BYTES = 20 * 2**20


def dot(a, b, ca, cb):
    return lax.dot_general(a, b, (((ca,), (cb,)), ((), ())), preferred_element_type=F32)


def activate(gate_pre, up_pre, down_grad):
    sigmoid_val = jax.nn.sigmoid(gate_pre)
    swish_val = gate_pre * sigmoid_val
    hidden = (swish_val * up_pre).astype(BF)
    slope_val = sigmoid_val * (1.0 + gate_pre * (1.0 - sigmoid_val))
    gate_grad = (down_grad * up_pre * slope_val).astype(BF)
    up_grad = (down_grad * swish_val).astype(BF)
    return hidden, gate_grad, up_grad


def call(body, outs, flops, args):
    in_specs = [
        pl.BlockSpec(memory_space=pltpu.SMEM if a.ndim == 1 else pltpu.VMEM) for a in args
    ]
    moved = sum(a.size * a.dtype.itemsize for a in (*args, *outs))
    return pl.pallas_call(
        body,
        out_shape=outs,
        in_specs=in_specs,
        out_specs=[pl.BlockSpec(memory_space=pltpu.VMEM) for _ in outs],
        compiler_params=pltpu.CompilerParams(vmem_limit_bytes=VMEM_BYTES),
        cost_estimate=pl.CostEstimate(flops=flops, bytes_accessed=moved, transcendentals=0),
    )(*args)


def by_expert(rows, expert, experts):
    return [jnp.where(expert == e, rows, jnp.zeros_like(rows)) for e in range(experts)]


def forward_body(lo, hi, core_ref, expert_ref, got_ref, wg_ref, wu_ref, wd_ref, keep_ref, give_ref):
    n_y, part, _ = keep_ref.shape
    experts = wg_ref.shape[0]
    _, _, own, cols = got_ref.shape
    width = hi - lo
    core = core_ref[0]
    pairs = ROWS // (2 * part)
    owners = ROWS // own

    @pl.loop(0, n_y // pairs)
    def _(i):
        expert = expert_ref[pl.ds(pl.multiple_of(i * ROWS, ROWS), ROWS), :]
        src = pl.ds(i * owners, owners)
        toks = by_expert(got_ref[src, 0].reshape(ROWS, cols), expert, experts)
        cots = by_expert(got_ref[src, 1].reshape(ROWS, cols), expert, experts)
        for k in range(3):
            out = 0.0
            for e in range(experts):
                if k < 2:
                    out = out + dot(toks[e], (wg_ref, wu_ref)[k][e, :, lo:hi], 1, 0)
                else:
                    out = out + dot(cots[e], wd_ref[e, lo:hi, :], 1, 1)
            to = slice(k * width, (k + 1) * width)
            for j in range(pairs):
                even = out[2 * j * part : (2 * j + 1) * part]
                odd = out[(2 * j + 1) * part : (2 * j + 2) * part]
                keep_ref[i * pairs + j, :, to] = jnp.where(core == 0, even, odd)
                give_ref[i * pairs + j, :, to] = jnp.where(core == 0, odd, even).astype(BF)


def terms(rows, expert, gate_ref, up_ref, lo, hi):
    experts, width = gate_ref.shape[0], hi - lo
    gates = by_expert(rows[:, :width], expert, experts)
    ups = by_expert(rows[:, width : 2 * width], expert, experts)
    out = 0.0
    for e in range(experts):
        out = out + dot(gates[e], gate_ref[e, :, lo:hi], 1, 1)
        out = out + dot(ups[e], up_ref[e, :, lo:hi], 1, 1)
    return out


def head_body(lo, hi, expert_ref, gate_ref, up_ref, grads_ref, out_ref):
    @pl.loop(0, out_ref.shape[0] // ROWS)
    def _(i):
        at = pl.ds(pl.multiple_of(i * ROWS, ROWS), ROWS)
        out_ref[at, :] = terms(grads_ref[at, :], expert_ref[at, :], gate_ref, up_ref, lo, hi)


def tail_body(lo, hi, core_ref, expert_ref, gate_ref, up_ref, head_ref, own_ref, other_ref, grads_ref, out_ref):
    n_y, n_core, part, width = grads_ref.shape
    core = core_ref[0]
    for i in range(n_y):
        grads_ref[i, core] = own_ref[i]
        grads_ref[i, 1 - core] = other_ref[i]
    per_y = n_core * part

    @pl.loop(0, out_ref.shape[0] // ROWS)
    def _(i):
        at = pl.ds(pl.multiple_of(i * ROWS, ROWS), ROWS)
        rows = grads_ref[pl.ds(i * (ROWS // per_y), ROWS // per_y)].reshape(ROWS, width)
        out = head_ref[at, :] + terms(rows, expert_ref[at, :], gate_ref, up_ref, lo, hi)
        out_ref[at, :] = out.astype(BF)


def total_body(x_ref, out_ref):
    out = x_ref[0].astype(F32)
    for i in range(1, x_ref.shape[0]):
        out = out + x_ref[i].astype(F32)
    out_ref[...] = out.astype(BF)


def make(n_y, n_core, n_x, n_z):
    dp, cuts = ("y", "core"), ("x", "z")
    n_dp, n_cuts = n_y * n_core, n_x * n_z
    swap = [(i, n_core - 1 - i) for i in range(n_core)]

    def per_device(tokens, cotangent, w_gate, w_up, w_down, row_token, block_expert, gate_weight):
        own, cols = tokens.shape
        n_tok = row_token.shape[0]
        experts, _, hid = w_gate.shape
        blk = n_tok // block_expert.shape[0]
        part = n_tok // n_dp
        core = lax.axis_index("core").astype(jnp.int32).reshape(1)
        work = 2 * n_tok * experts * cols

        def exchange(v, axes):
            return lax.all_to_all(v, axes, split_axis=0, concat_axis=0, tiled=True)

        def spread(v, n):
            return jnp.broadcast_to(v[None], (n,) + v.shape)

        first = (lax.axis_index("x") * n_z + lax.axis_index("z")) * own
        holds_own = row_token[None, :] == first + jnp.arange(own, dtype=jnp.int32)[:, None]
        weight_own = jnp.sum(jnp.where(holds_own, gate_weight[None, :], 0.0), axis=1)
        expert_row = jnp.repeat(block_expert[:, 0], blk)
        holds = row_token[None, :] == jnp.arange(n_tok, dtype=jnp.int32)[:, None]
        expert_tok = jnp.sum(jnp.where(holds, expert_row[None, :], 0), axis=1)[:, None]

        cot_own = (cotangent.astype(F32) * weight_own[:, None]).astype(BF)
        got = exchange(spread(jnp.stack([tokens, cot_own]), n_cuts), cuts)

        def partial(lo, hi):
            shape = (n_y, part, 3 * (hi - lo))
            outs = [jax.ShapeDtypeStruct(shape, F32), jax.ShapeDtypeStruct(shape, BF)]
            args = (core, expert_tok, got, w_gate, w_up, w_down)
            keep, give = call(functools.partial(forward_body, lo, hi), outs, work * 3 * (hi - lo), args)
            came = lax.ppermute(give, "core", swap)
            return (keep + came.astype(F32)).astype(BF)

        def total(chip):
            pre = jnp.sum(exchange(chip, "y").astype(F32), axis=0)
            width = pre.shape[1] // 3
            hidden, gate_grad, up_grad = activate(
                pre[:, :width], pre[:, width : 2 * width], pre[:, 2 * width :]
            )
            return jnp.concatenate([gate_grad, up_grad, hidden], axis=1)

        chip_a, chip_b = partial(0, CUT), partial(CUT, hid)
        act_a = lax.all_gather(total(chip_a), dp, axis=0, tiled=True)
        act_b = exchange(spread(total(chip_b), n_y), "y")
        act_o = lax.ppermute(act_b, "core", swap)

        outs = [jax.ShapeDtypeStruct((n_tok, cols), F32)]
        args = (expert_tok, w_gate, w_up, act_a)
        (terms_a,) = call(functools.partial(head_body, 0, CUT), outs, 2 * work * CUT, args)
        outs = [
            jax.ShapeDtypeStruct((n_y, n_core, part, act_b.shape[2]), BF),
            jax.ShapeDtypeStruct((n_tok, cols), BF),
        ]
        args = (core, expert_tok, w_gate, w_up, terms_a, act_b, act_o)
        body = functools.partial(tail_body, CUT, hid)
        act_b, both = call(body, outs, 2 * work * (hid - CUT), args)
        act_b = act_b.reshape(n_tok, -1)
        both = exchange(both.reshape(n_cuts, own, cols), cuts)
        outs = [jax.ShapeDtypeStruct((own, cols), BF)]
        (token_grad,) = call(total_body, outs, both.size, (both,))

        def joined(k):
            rest = hid - CUT
            halves = [act_a[:, k * CUT : (k + 1) * CUT], act_b[:, k * rest : (k + 1) * rest]]
            return jnp.concatenate(halves, axis=1)

        tok, cot = got[:, 0].reshape(n_tok, cols), got[:, 1].reshape(n_tok, cols)
        masks = [expert_tok == e for e in range(experts)]
        tok_by = jnp.concatenate([jnp.where(m, tok, 0) for m in masks], axis=1)
        grad_gate = dot(tok_by, joined(0), 0, 0).astype(BF).reshape(w_gate.shape)
        grad_up = dot(tok_by, joined(1), 0, 0).astype(BF).reshape(w_up.shape)
        hidden = joined(2)
        grad_down = [dot(hidden, jnp.where(m, cot, 0), 0, 0).astype(BF) for m in masks]
        return token_grad, grad_gate, grad_up, jnp.stack(grad_down)

    return per_device


def solution(mesh):
    n_y, n_core, n_x, n_z = 8, 2, 4, 8
    fine = Mesh(mesh.devices.reshape(n_y, n_core, n_x, n_z), ("y", "core", "x", "z"))
    dp, cuts = ("y", "core"), ("x", "z")
    return jax.shard_map(
        make(n_y, n_core, n_x, n_z),
        mesh=fine,
        in_specs=(
            P(cuts, dp),
            P(cuts, dp),
            P(None, dp, cuts),
            P(None, dp, cuts),
            P(None, cuts, dp),
            P(),
            P(),
            P(),
        ),
        out_specs=(P(cuts, dp), P(None, dp, cuts), P(None, dp, cuts), P(None, cuts, dp)),
        check_vma=False,
    )
```

```python
import functools

import jax
import jax.numpy as jnp
from jax import lax
from jax.experimental import pallas as pl
from jax.experimental.pallas import tpu as pltpu
from jax.sharding import Mesh
from jax.sharding import PartitionSpec as P

BF = jnp.bfloat16
F32 = jnp.float32
ROWS = 256
VMEM_BYTES = 20 * 2**20


def dot(a, b, ca, cb):
    return lax.dot_general(a, b, (((ca,), (cb,)), ((), ())), preferred_element_type=F32)


def activate(gate_pre, up_pre, down_grad):
    sigmoid_val = jax.nn.sigmoid(gate_pre)
    swish_val = gate_pre * sigmoid_val
    hidden = (swish_val * up_pre).astype(BF)
    slope_val = sigmoid_val * (1.0 + gate_pre * (1.0 - sigmoid_val))
    gate_grad = (down_grad * up_pre * slope_val).astype(BF)
    up_grad = (down_grad * swish_val).astype(BF)
    return hidden, gate_grad, up_grad


def call(body, outs, flops, args):
    spaces = [pltpu.SMEM if a.ndim == 1 else pltpu.VMEM for a in args]
    in_specs = [pl.BlockSpec(memory_space=space) for space in spaces]
    moved = sum(a.size * a.dtype.itemsize for a in (*args, *outs))
    return pl.pallas_call(
        body,
        out_shape=outs,
        in_specs=in_specs,
        out_specs=[pl.BlockSpec(memory_space=pltpu.VMEM) for _ in outs],
        compiler_params=pltpu.CompilerParams(vmem_limit_bytes=VMEM_BYTES),
        cost_estimate=pl.CostEstimate(flops=flops, bytes_accessed=moved, transcendentals=0),
    )(*args)


def by_expert(rows, expert, experts):
    return [jnp.where(expert == e, rows, jnp.zeros_like(rows)) for e in range(experts)]


def forward_body(at_ref, expert_ref, got_ref, wg_ref, wu_ref, wd_ref, keep_ref, give_ref):
    _, n_yh, part, width = keep_ref.shape
    experts = wg_ref.shape[0]
    _, _, own, cols = got_ref.shape
    hid = width // 3
    parity, core = at_ref[0], at_ref[1]
    owners = ROWS // own
    for k, w_ref in enumerate((wg_ref, wu_ref, wd_ref)):
        side, cb = k // 2, k // 2
        to = slice(k * hid, (k + 1) * hid)

        @pl.loop(0, n_yh)
        def _(i):
            expert = expert_ref[pl.ds(pl.multiple_of(i * ROWS, ROWS), ROWS), :]
            rows = got_ref[pl.ds(i * owners, owners), side].reshape(ROWS, cols)
            out = 0.0
            for e, x in enumerate(by_expert(rows, expert, experts)):
                out = out + dot(x, w_ref[e], 1, cb)
            for p in range(2):
                even = out[2 * p * part : (2 * p + 1) * part]
                odd = out[(2 * p + 1) * part : (2 * p + 2) * part]
                slot = lax.rem(parity + p, 2)
                keep_ref[slot, i, :, to] = jnp.where(core == 0, even, odd)
                give_ref[slot, i, :, to] = jnp.where(core == 0, odd, even).astype(BF)


def terms_body(at_ref, expert_ref, gate_ref, up_ref, mine_ref, other_ref, grads_ref, out_ref):
    n_yh, n_yl, n_core, part, width = grads_ref.shape
    experts, _, hid = gate_ref.shape
    parity, core = at_ref[0], at_ref[1]

    @pl.loop(0, n_yh)
    def _(i):
        for p in range(n_yl):
            grads_ref[i, lax.rem(parity + p, 2), core] = mine_ref[p, i]
            grads_ref[i, lax.rem(parity + p, 2), 1 - core] = other_ref[p, i]
        at = pl.ds(pl.multiple_of(i * ROWS, ROWS), ROWS)
        expert = expert_ref[at, :]
        rows = grads_ref[i].reshape(ROWS, width)
        gates = by_expert(rows[:, :hid], expert, experts)
        ups = by_expert(rows[:, hid:], expert, experts)
        out = 0.0
        for e in range(experts):
            out = out + dot(gates[e], gate_ref[e], 1, 1) + dot(ups[e], up_ref[e], 1, 1)
        out_ref[at, :] = out.astype(BF)


def total_body(x_ref, out_ref):
    out = x_ref[0].astype(F32)
    for i in range(1, x_ref.shape[0]):
        out = out + x_ref[i].astype(F32)
    out_ref[...] = out.astype(BF)


def make(n_yh, n_yl, n_core, n_x, n_z):
    along_y, dp, cuts = ("yh", "yl"), ("yh", "yl", "core"), ("x", "z")
    n_y = n_yh * n_yl
    n_dp, n_cuts = n_y * n_core, n_x * n_z
    swap = [(i, n_core - 1 - i) for i in range(n_core)]
    left = [(i, i ^ 1) for i in range(n_y)]
    right = [(i, (i + 1) % n_y if i % 2 else (i - 1) % n_y) for i in range(n_y)]

    def per_device(tokens, cotangent, w_gate, w_up, w_down, row_token, block_expert, gate_weight):
        own, cols = tokens.shape
        n_tok = row_token.shape[0]
        experts, _, hid = w_gate.shape
        blk = n_tok // block_expert.shape[0]
        part = n_tok // n_dp
        at = jnp.stack([lax.axis_index("yl"), lax.axis_index("core")]).astype(jnp.int32)
        work = 2 * n_tok * experts * cols * hid

        def exchange(v, axes):
            return lax.all_to_all(v, axes, split_axis=0, concat_axis=0, tiled=True)

        def spread(v, n):
            return jnp.broadcast_to(v[None], (n,) + v.shape)

        def neighbours(v):
            half = v.shape[-1] // 2
            return (
                lax.ppermute(v[..., :half], along_y, left),
                lax.ppermute(v[..., half:], along_y, right),
            )

        first = (lax.axis_index("x") * n_z + lax.axis_index("z")) * own
        holds_own = row_token[None, :] == first + jnp.arange(own, dtype=jnp.int32)[:, None]
        weight_own = jnp.sum(jnp.where(holds_own, gate_weight[None, :], 0.0), axis=1)
        expert_row = jnp.repeat(block_expert[:, 0], blk)
        holds = row_token[None, :] == jnp.arange(n_tok, dtype=jnp.int32)[:, None]
        expert_tok = jnp.sum(jnp.where(holds, expert_row[None, :], 0), axis=1)[:, None]

        cot_own = (cotangent.astype(F32) * weight_own[:, None]).astype(BF)
        got = exchange(spread(jnp.stack([tokens, cot_own]), n_z), "z")
        got = exchange(spread(got.reshape(n_z, 2, own, cols), n_x), "x")
        got = got.reshape(n_cuts, 2, own, cols)

        shape = (n_yl, n_yh, part, 3 * hid)
        outs = [jax.ShapeDtypeStruct(shape, F32), jax.ShapeDtypeStruct(shape, BF)]
        args = (at, expert_tok, got, w_gate, w_up, w_down)
        keep, give = call(forward_body, outs, 3 * work, args)
        came = lax.ppermute(give, "core", swap)
        near = neighbours((keep[1] + came[1].astype(F32)).astype(BF))
        near = jnp.concatenate(near, axis=-1)
        chips = (keep[0] + came[0].astype(F32) + near.astype(F32)).astype(BF)
        pre = jnp.sum(exchange(chips, "yh").astype(F32), axis=0)
        hidden, gate_grad, up_grad = activate(
            pre[:, :hid], pre[:, hid : 2 * hid], pre[:, 2 * hid :]
        )
        hidden = lax.all_gather(hidden, dp, axis=0, tiled=True)
        grads = exchange(spread(jnp.concatenate([gate_grad, up_grad], axis=1), n_yh), "yh")
        grads = grads.reshape(n_yh, part, 2 * hid)
        mine = jnp.stack([grads, jnp.concatenate(neighbours(grads), axis=-1)])
        other = lax.ppermute(mine, "core", swap)

        outs = [
            jax.ShapeDtypeStruct((n_yh, n_yl, n_core, part, 2 * hid), BF),
            jax.ShapeDtypeStruct((n_tok, cols), BF),
        ]
        args = (at, expert_tok, w_gate, w_up, mine, other)
        grads, terms = call(terms_body, outs, 2 * work, args)
        grads, hidden = lax.optimization_barrier((grads.reshape(n_tok, 2 * hid), hidden))
        terms = exchange(terms.reshape(n_cuts, own, cols), cuts)
        outs = [jax.ShapeDtypeStruct((own, cols), BF)]
        (token_grad,) = call(total_body, outs, terms.size, (terms,))

        tok, cot = got[:, 0].reshape(n_tok, cols), got[:, 1].reshape(n_tok, cols)
        masks = [expert_tok == e for e in range(experts)]
        tok_by = jnp.concatenate([jnp.where(m, tok, 0) for m in masks], axis=1)
        grad_gate = dot(tok_by, grads[:, :hid], 0, 0).astype(BF).reshape(w_gate.shape)
        grad_up = dot(tok_by, grads[:, hid:], 0, 0).astype(BF).reshape(w_up.shape)
        grad_down = [dot(hidden, jnp.where(m, cot, 0), 0, 0).astype(BF) for m in masks]
        return token_grad, grad_gate, grad_up, jnp.stack(grad_down)

    return per_device


def solution(mesh):
    sizes, axes = (4, 2, 2, 4, 8), ("yh", "yl", "core", "x", "z")
    fine = Mesh(mesh.devices.reshape(sizes), axes)
    dp, cuts = ("yh", "yl", "core"), ("x", "z")
    return jax.shard_map(
        make(*sizes),
        mesh=fine,
        in_specs=(
            P(cuts, dp),
            P(cuts, dp),
            P(None, dp, cuts),
            P(None, dp, cuts),
            P(None, cuts, dp),
            P(),
            P(),
            P(),
        ),
        out_specs=(P(cuts, dp), P(None, dp, cuts), P(None, dp, cuts), P(None, cuts, dp)),
        check_vma=False,
    )
```

```python
import functools

import jax
import jax.numpy as jnp
from jax import lax
from jax.experimental import pallas as pl
from jax.experimental.pallas import tpu as pltpu
from jax.sharding import Mesh
from jax.sharding import PartitionSpec as P

BF = jnp.bfloat16
F32 = jnp.float32
ROWS = 256
VMEM_BYTES = 20 * 2**20


def dot(a, b, ca, cb):
    return lax.dot_general(a, b, (((ca,), (cb,)), ((), ())), preferred_element_type=F32)


def activate(gate_pre, up_pre, down_grad):
    sigmoid_val = jax.nn.sigmoid(gate_pre)
    swish_val = gate_pre * sigmoid_val
    hidden = (swish_val * up_pre).astype(BF)
    slope_val = sigmoid_val * (1.0 + gate_pre * (1.0 - sigmoid_val))
    gate_grad = (down_grad * up_pre * slope_val).astype(BF)
    up_grad = (down_grad * swish_val).astype(BF)
    return hidden, gate_grad, up_grad


def call(body, outs, flops, args):
    spaces = [pltpu.SMEM if a.ndim == 1 else pltpu.VMEM for a in args]
    in_specs = [pl.BlockSpec(memory_space=space) for space in spaces]
    moved = sum(a.size * a.dtype.itemsize for a in (*args, *outs))
    return pl.pallas_call(
        body,
        out_shape=outs,
        in_specs=in_specs,
        out_specs=[pl.BlockSpec(memory_space=pltpu.VMEM) for _ in outs],
        compiler_params=pltpu.CompilerParams(vmem_limit_bytes=VMEM_BYTES),
        cost_estimate=pl.CostEstimate(flops=flops, bytes_accessed=moved, transcendentals=0),
    )(*args)


def by_expert(rows, expert, experts):
    return [jnp.where(expert == e, rows, jnp.zeros_like(rows)) for e in range(experts)]


def forward_body(side, at_ref, expert_ref, got_ref, wg_ref, wu_ref, wd_ref, keep_ref, give_ref):
    n_yh, part, width = keep_ref.shape
    experts = wg_ref.shape[0]
    _, _, own, cols = got_ref.shape
    hid = width // 3
    parity, core = lax.rem(at_ref[0] + side, 2), at_ref[1]
    per = 2 * part
    owners = per // own
    group = ROWS // per

    @pl.loop(0, n_yh // group)
    def _(i):
        starts = [2 * (i * group + q) + parity for q in range(group)]
        expert = jnp.concatenate(
            [expert_ref[pl.ds(pl.multiple_of(s * per, per), per), :] for s in starts]
        )
        masked = []
        for kind in range(2):
            rows = [got_ref[pl.ds(s * owners, owners), kind].reshape(per, cols) for s in starts]
            masked.append(by_expert(jnp.concatenate(rows), expert, experts))
        for k, w_ref in enumerate((wg_ref, wu_ref, wd_ref)):
            out = 0.0
            for e in range(experts):
                out = out + dot(masked[k // 2][e], w_ref[e], 1, k // 2)
            to = slice(k * hid, (k + 1) * hid)
            for q in range(group):
                even = out[q * per : q * per + part]
                odd = out[q * per + part : (q + 1) * per]
                keep_ref[i * group + q, :, to] = jnp.where(core == 0, even, odd)
                give_ref[i * group + q, :, to] = jnp.where(core == 0, odd, even).astype(BF)


def terms_body(side, at_ref, expert_ref, gate_ref, up_ref, mine_ref, other_ref, *refs):
    out_ref = refs[-1]
    n_yh, part, width = mine_ref.shape
    experts, _, hid = gate_ref.shape
    parity, core = lax.rem(at_ref[0] + side, 2), at_ref[1]
    per = 2 * part
    group = ROWS // per

    @pl.loop(0, n_yh // group)
    def _(i):
        expert, rows = [], []
        for q in range(group):
            start = (2 * (i * group + q) + parity) * per
            expert.append(expert_ref[pl.ds(pl.multiple_of(start, per), per), :])
            mine, other = mine_ref[i * group + q], other_ref[i * group + q]
            rows += [jnp.where(core == 0, mine, other), jnp.where(core == 0, other, mine)]
        expert, rows = jnp.concatenate(expert), jnp.concatenate(rows)
        gates = by_expert(rows[:, :hid], expert, experts)
        ups = by_expert(rows[:, hid:], expert, experts)
        out = 0.0
        for e in range(experts):
            out = out + dot(gates[e], gate_ref[e], 1, 1) + dot(ups[e], up_ref[e], 1, 1)
        out = out.astype(BF)
        for q in range(group):
            piece = out[q * per : (q + 1) * per]
            if side:
                out_ref[i * group + q, parity] = piece
                out_ref[i * group + q, 1 - parity] = refs[0][i * group + q]
            else:
                out_ref[i * group + q] = piece


def order_body(at_ref, mine_ref, other_ref, far_mine_ref, far_other_ref, out_ref):
    parity, core = at_ref[0], at_ref[1]

    @pl.loop(0, mine_ref.shape[0])
    def _(i):
        out_ref[i, parity, core] = mine_ref[i]
        out_ref[i, parity, 1 - core] = other_ref[i]
        out_ref[i, 1 - parity, core] = far_mine_ref[i]
        out_ref[i, 1 - parity, 1 - core] = far_other_ref[i]


def total_body(x_ref, out_ref):
    out = x_ref[0].astype(F32)
    for i in range(1, x_ref.shape[0]):
        out = out + x_ref[i].astype(F32)
    out_ref[...] = out.astype(BF)


def make(n_yh, n_yl, n_core, n_x, n_z):
    along_y, dp, cuts = ("yh", "yl"), ("yh", "yl", "core"), ("x", "z")
    n_y = n_yh * n_yl
    n_dp, n_cuts = n_y * n_core, n_x * n_z
    swap = [(i, n_core - 1 - i) for i in range(n_core)]
    left = [(i, i ^ 1) for i in range(n_y)]
    right = [(i, (i + 1) % n_y if i % 2 else (i - 1) % n_y) for i in range(n_y)]

    def per_device(tokens, cotangent, w_gate, w_up, w_down, row_token, block_expert, gate_weight):
        own, cols = tokens.shape
        n_tok = row_token.shape[0]
        experts, _, hid = w_gate.shape
        blk = n_tok // block_expert.shape[0]
        part = n_tok // n_dp
        at = jnp.stack([lax.axis_index("yl"), lax.axis_index("core")]).astype(jnp.int32)
        work = 2 * n_tok * experts * cols * hid

        def exchange(v, axes):
            return lax.all_to_all(v, axes, split_axis=0, concat_axis=0, tiled=True)

        def spread(v, n):
            return jnp.broadcast_to(v[None], (n,) + v.shape)

        def halves(v):
            half = v.shape[-1] // 2
            return v[..., :half], v[..., half:]

        def neighbours(v):
            return lax.ppermute(v[0], along_y, left), lax.ppermute(v[1], along_y, right)

        first = (lax.axis_index("x") * n_z + lax.axis_index("z")) * own
        holds_own = row_token[None, :] == first + jnp.arange(own, dtype=jnp.int32)[:, None]
        weight_own = jnp.sum(jnp.where(holds_own, gate_weight[None, :], 0.0), axis=1)
        expert_row = jnp.repeat(block_expert[:, 0], blk)
        holds = row_token[None, :] == jnp.arange(n_tok, dtype=jnp.int32)[:, None]
        expert_tok = jnp.sum(jnp.where(holds, expert_row[None, :], 0), axis=1)[:, None]

        cot_own = (cotangent.astype(F32) * weight_own[:, None]).astype(BF)
        got = exchange(spread(jnp.stack([tokens, cot_own]), n_z), "z")
        got = exchange(spread(got.reshape(n_z, 2, own, cols), n_x), "x")
        got = got.reshape(n_cuts, 2, own, cols)

        shape = (n_yh, part, 3 * hid)
        outs = [jax.ShapeDtypeStruct(shape, F32), jax.ShapeDtypeStruct(shape, BF)]

        def forward(side):
            args = (at, expert_tok, got, w_gate, w_up, w_down)
            return call(functools.partial(forward_body, side), outs, 3 * work // 2, args)

        far_keep, far_give = forward(1)
        far_came = lax.ppermute(far_give, "core", swap)
        keep, give = forward(0)
        far = halves((far_keep + far_came.astype(F32)).astype(BF))
        far, give = lax.optimization_barrier((far, give))
        near = neighbours(far)
        came = lax.ppermute(give, "core", swap)
        chips = keep + came.astype(F32) + jnp.concatenate(near, axis=-1).astype(F32)
        chips = chips.astype(BF)
        pre = jnp.sum(exchange(chips, "yh").astype(F32), axis=0)
        hidden, gate_grad, up_grad = activate(
            pre[:, :hid], pre[:, hid : 2 * hid], pre[:, 2 * hid :]
        )
        hidden = lax.all_gather(hidden, dp, axis=0, tiled=True)
        grads = exchange(spread(jnp.concatenate([gate_grad, up_grad], axis=1), n_yh), "yh")
        grads = grads.reshape(n_yh, part, 2 * hid)
        near = neighbours(halves(grads))
        other = lax.ppermute(grads, "core", swap)
        outs = [jax.ShapeDtypeStruct((n_yh, n_core * part, cols), BF)]
        args = (at, expert_tok, w_gate, w_up, grads, other)
        (own_terms,) = call(functools.partial(terms_body, 0), outs, work, args)
        far = jnp.concatenate(near, axis=-1)
        far_other = lax.ppermute(far, "core", swap)
        outs = [jax.ShapeDtypeStruct((n_yh, n_yl, n_core * part, cols), BF)]
        args = (at, expert_tok, w_gate, w_up, far, far_other, own_terms)
        (terms,) = call(functools.partial(terms_body, 1), outs, work, args)
        terms = exchange(terms.reshape(n_cuts, own, cols), cuts)
        outs = [jax.ShapeDtypeStruct((own, cols), BF)]
        (token_grad,) = call(total_body, outs, terms.size, (terms,))

        outs = [jax.ShapeDtypeStruct((n_yh, n_yl, n_core, part, 2 * hid), BF)]
        (grads,) = call(order_body, outs, grads.size, (at, grads, other, far, far_other))
        grads = grads.reshape(n_tok, 2 * hid)
        tok, cot = got[:, 0].reshape(n_tok, cols), got[:, 1].reshape(n_tok, cols)
        masks = [expert_tok == e for e in range(experts)]
        tok_by = jnp.concatenate([jnp.where(m, tok, 0) for m in masks], axis=1)
        grad_gate = dot(tok_by, grads[:, :hid], 0, 0).astype(BF).reshape(w_gate.shape)
        grads, hidden = lax.optimization_barrier((grads, hidden))
        grad_up = dot(tok_by, grads[:, hid:], 0, 0).astype(BF).reshape(w_up.shape)
        grad_down = [dot(hidden, jnp.where(m, cot, 0), 0, 0).astype(BF) for m in masks]
        return token_grad, grad_gate, grad_up, jnp.stack(grad_down)

    return per_device


def solution(mesh):
    sizes, axes = (4, 2, 2, 4, 8), ("yh", "yl", "core", "x", "z")
    fine = Mesh(mesh.devices.reshape(sizes), axes)
    dp, cuts = ("yh", "yl", "core"), ("x", "z")
    return jax.shard_map(
        make(*sizes),
        mesh=fine,
        in_specs=(
            P(cuts, dp),
            P(cuts, dp),
            P(None, dp, cuts),
            P(None, dp, cuts),
            P(None, cuts, dp),
            P(),
            P(),
            P(),
        ),
        out_specs=(P(cuts, dp), P(None, dp, cuts), P(None, dp, cuts), P(None, cuts, dp)),
        check_vma=False,
    )
```

```python
import functools

import jax
import jax.numpy as jnp
from jax import lax
from jax.experimental import pallas as pl
from jax.experimental.pallas import tpu as pltpu
from jax.sharding import Mesh
from jax.sharding import PartitionSpec as P

BF = jnp.bfloat16
F32 = jnp.float32
ROWS = 256
VMEM_BYTES = 14 * 2**20


def dot(a, b, ca, cb):
    return lax.dot_general(a, b, (((ca,), (cb,)), ((), ())), preferred_element_type=F32)


def activate(gate_pre, up_pre, down_grad):
    sigmoid_val = jax.nn.sigmoid(gate_pre)
    swish_val = gate_pre * sigmoid_val
    hidden = (swish_val * up_pre).astype(BF)
    slope_val = sigmoid_val * (1.0 + gate_pre * (1.0 - sigmoid_val))
    gate_grad = (down_grad * up_pre * slope_val).astype(BF)
    up_grad = (down_grad * swish_val).astype(BF)
    return hidden, gate_grad, up_grad


def call(body, outs, flops, args):
    spaces = [pltpu.SMEM if a.ndim == 1 else pltpu.VMEM for a in args]
    in_specs = [pl.BlockSpec(memory_space=space) for space in spaces]
    moved = sum(a.size * a.dtype.itemsize for a in (*args, *outs))
    return pl.pallas_call(
        body,
        out_shape=outs,
        in_specs=in_specs,
        out_specs=[pl.BlockSpec(memory_space=pltpu.VMEM) for _ in outs],
        compiler_params=pltpu.CompilerParams(vmem_limit_bytes=VMEM_BYTES),
        cost_estimate=pl.CostEstimate(flops=flops, bytes_accessed=moved, transcendentals=0),
    )(*args)


def by_expert(rows, expert, experts):
    return [jnp.where(expert == e, rows, jnp.zeros_like(rows)) for e in range(experts)]


def forward_body(side, at_ref, expert_ref, got_ref, pair_ref, wd_ref, keep_ref, *give_refs):
    n_yh, part, width = keep_ref.shape
    experts = wd_ref.shape[0]
    _, _, own, cols = got_ref.shape
    hid = width // 3
    parity, core = lax.rem(at_ref[0] + side, 2), at_ref[1]
    per = 2 * part
    owners = per // own
    group = ROWS // per

    @pl.loop(0, n_yh // group)
    def _(i):
        starts = [2 * (i * group + q) + parity for q in range(group)]
        expert = jnp.concatenate(
            [expert_ref[pl.ds(pl.multiple_of(s * per, per), per), :] for s in starts]
        )
        masked = []
        for kind in range(2):
            rows = [got_ref[pl.ds(s * owners, owners), kind].reshape(per, cols) for s in starts]
            masked.append(by_expert(jnp.concatenate(rows), expert, experts))
        for k in range(3):
            w_ref = wd_ref if k == 2 else pair_ref.at[k]
            out = 0.0
            for e in range(experts):
                out = out + dot(masked[k // 2][e], w_ref[e], 1, k // 2)
            to = slice(k * hid, (k + 1) * hid)
            for q in range(group):
                even = out[q * per : q * per + part]
                odd = out[q * per + part : (q + 1) * per]
                keep_ref[i * group + q, :, to] = jnp.where(core == 0, even, odd)
                give = jnp.where(core == 0, odd, even).astype(BF)
                if len(give_refs) == 1:
                    give_refs[0][i * group + q, :, to] = give
                else:
                    give_refs[k][i * group + q] = give


def terms_body(side, at_ref, expert_ref, pair_ref, mine_ref, other_ref, *refs):
    out_ref = refs[-1]
    n_yh, part, width = mine_ref.shape
    _, experts, _, hid = pair_ref.shape
    parity, core = lax.rem(at_ref[0] + side, 2), at_ref[1]
    per = 2 * part
    group = ROWS // per

    @pl.loop(0, n_yh // group)
    def _(i):
        expert, rows = [], []
        for q in range(group):
            start = (2 * (i * group + q) + parity) * per
            expert.append(expert_ref[pl.ds(pl.multiple_of(start, per), per), :])
            mine, other = mine_ref[i * group + q], other_ref[i * group + q]
            rows += [jnp.where(core == 0, mine, other), jnp.where(core == 0, other, mine)]
        expert, rows = jnp.concatenate(expert), jnp.concatenate(rows)
        gates = by_expert(rows[:, :hid], expert, experts)
        ups = by_expert(rows[:, hid:], expert, experts)
        out = 0.0
        for e in range(experts):
            out = out + dot(gates[e], pair_ref[0, e], 1, 1) + dot(ups[e], pair_ref[1, e], 1, 1)
        out = out.astype(BF)
        for q in range(group):
            piece = out[q * per : (q + 1) * per]
            if side:
                out_ref[i * group + q, parity] = piece
                out_ref[i * group + q, 1 - parity] = refs[0][i * group + q]
            else:
                out_ref[i * group + q] = piece


def order_body(at_ref, mine_ref, other_ref, far_mine_ref, far_other_ref, out_ref):
    parity, core = at_ref[0], at_ref[1]

    @pl.loop(0, mine_ref.shape[0])
    def _(i):
        out_ref[i, parity, core] = mine_ref[i]
        out_ref[i, parity, 1 - core] = other_ref[i]
        out_ref[i, 1 - parity, core] = far_mine_ref[i]
        out_ref[i, 1 - parity, 1 - core] = far_other_ref[i]


def total_body(x_ref, out_ref):
    out = x_ref[0].astype(F32)
    for i in range(1, x_ref.shape[0]):
        out = out + x_ref[i].astype(F32)
    out_ref[...] = out.astype(BF)


def make(n_yh, n_yl, n_core, n_x, n_z):
    along_y, dp, cuts = ("yh", "yl"), ("yh", "yl", "core"), ("x", "z")
    n_y = n_yh * n_yl
    n_dp, n_cuts = n_y * n_core, n_x * n_z
    swap = [(i, n_core - 1 - i) for i in range(n_core)]
    left = [(i, i ^ 1) for i in range(n_y)]
    right = [(i, (i + 1) % n_y if i % 2 else (i - 1) % n_y) for i in range(n_y)]

    def per_device(tokens, cotangent, w_gate, w_up, w_down, row_token, block_expert, gate_weight):
        own, cols = tokens.shape
        n_tok = row_token.shape[0]
        experts, _, hid = w_gate.shape
        blk = n_tok // block_expert.shape[0]
        part = n_tok // n_dp
        at = jnp.stack([lax.axis_index("yl"), lax.axis_index("core")]).astype(jnp.int32)
        work = 2 * n_tok * experts * cols * hid

        def exchange(v, axes):
            return lax.all_to_all(v, axes, split_axis=0, concat_axis=0, tiled=True)

        def spread(v, n):
            return jnp.broadcast_to(v[None], (n,) + v.shape)

        def halves(v):
            half = v.shape[-1] // 2
            return v[..., :half], v[..., half:]

        def neighbours(v):
            return lax.ppermute(v[0], along_y, left), lax.ppermute(v[1], along_y, right)

        first = (lax.axis_index("x") * n_z + lax.axis_index("z")) * own
        expert_row = jnp.repeat(block_expert[:, 0], blk)
        holds = row_token[None, :] == jnp.arange(n_tok, dtype=jnp.int32)[:, None]
        expert_tok = jnp.sum(jnp.where(holds, expert_row[None, :], 0), axis=1)[:, None]

        holds_own = row_token[None, :] == first + jnp.arange(own, dtype=jnp.int32)[:, None]
        weight_own = jnp.sum(jnp.where(holds_own, gate_weight[None, :], 0.0), axis=1)
        cot_own = (cotangent.astype(F32) * weight_own[:, None]).astype(BF)
        got = exchange(spread(jnp.stack([tokens, cot_own]), n_z), "z")
        pair = jnp.stack([w_gate, w_up])
        got = exchange(spread(got.reshape(n_z, 2, own, cols), n_x), "x")
        got = got.reshape(n_cuts, 2, own, cols)

        def forward(side, pieces):
            width = 3 * hid // pieces
            outs = [jax.ShapeDtypeStruct((n_yh, part, 3 * hid), F32)]
            outs += [jax.ShapeDtypeStruct((n_yh, part, width), BF)] * pieces
            args = (at, expert_tok, got, pair, w_down)
            return call(functools.partial(forward_body, side), outs, 3 * work // 2, args)

        far_keep, far_give = forward(1, 1)
        far_came = lax.ppermute(far_give, "core", swap)
        keep, *give = forward(0, 3)
        far = halves((far_keep + far_came.astype(F32)).astype(BF))
        far, give = lax.optimization_barrier((far, give))
        near = neighbours(far)
        came = jnp.concatenate([lax.ppermute(g, "core", swap) for g in give], axis=-1)
        chips = keep + came.astype(F32) + jnp.concatenate(near, axis=-1).astype(F32)
        chips = chips.astype(BF)
        pre = jnp.sum(exchange(chips, "yh").astype(F32), axis=0)
        hidden, gate_grad, up_grad = activate(
            pre[:, :hid], pre[:, hid : 2 * hid], pre[:, 2 * hid :]
        )
        hidden = lax.all_gather(hidden, dp, axis=0, tiled=True)
        grads = exchange(spread(jnp.concatenate([gate_grad, up_grad], axis=1), n_yh), "yh")
        grads = grads.reshape(n_yh, part, 2 * hid)
        near = neighbours(halves(grads))
        other = lax.ppermute(grads, "core", swap)
        outs = [jax.ShapeDtypeStruct((n_yh, n_core * part, cols), BF)]
        args = (at, expert_tok, pair, grads, other)
        (own_terms,) = call(functools.partial(terms_body, 0), outs, work, args)
        far = jnp.concatenate(near, axis=-1)
        far_other = lax.ppermute(far, "core", swap)
        outs = [jax.ShapeDtypeStruct((n_yh, n_yl, n_core * part, cols), BF)]
        args = (at, expert_tok, pair, far, far_other, own_terms)
        (terms,) = call(functools.partial(terms_body, 1), outs, work, args)
        terms = exchange(terms.reshape(n_cuts, own, cols), cuts)
        outs = [jax.ShapeDtypeStruct((own, cols), BF)]
        (token_grad,) = call(total_body, outs, terms.size, (terms,))

        outs = [jax.ShapeDtypeStruct((n_yh, n_yl, n_core, part, 2 * hid), BF)]
        (grads,) = call(order_body, outs, grads.size, (at, grads, other, far, far_other))
        grads = grads.reshape(n_tok, 2 * hid)
        tok, cot = got[:, 0].reshape(n_tok, cols), got[:, 1].reshape(n_tok, cols)
        masks = [expert_tok == e for e in range(experts)]
        tok_by = jnp.concatenate([jnp.where(m, tok, 0) for m in masks], axis=1)
        grad_gate = dot(tok_by, grads[:, :hid], 0, 0).astype(BF).reshape(w_gate.shape)
        grads, hidden = lax.optimization_barrier((grads, hidden))
        grad_up = dot(tok_by, grads[:, hid:], 0, 0).astype(BF).reshape(w_up.shape)
        grad_down = [dot(hidden, jnp.where(m, cot, 0), 0, 0).astype(BF) for m in masks]
        return token_grad, grad_gate, grad_up, jnp.stack(grad_down)

    return per_device


def solution(mesh):
    sizes, axes = (4, 2, 2, 4, 8), ("yh", "yl", "core", "x", "z")
    fine = Mesh(mesh.devices.reshape(sizes), axes)
    dp, cuts = ("yh", "yl", "core"), ("x", "z")
    return jax.shard_map(
        make(*sizes),
        mesh=fine,
        in_specs=(
            P(cuts, dp),
            P(cuts, dp),
            P(None, dp, cuts),
            P(None, dp, cuts),
            P(None, cuts, dp),
            P(),
            P(),
            P(),
        ),
        out_specs=(P(cuts, dp), P(None, dp, cuts), P(None, dp, cuts), P(None, cuts, dp)),
        check_vma=False,
    )
```

```python
import functools

import jax
import jax.numpy as jnp
from jax import lax
from jax.experimental import pallas as pl
from jax.experimental.pallas import tpu as pltpu
from jax.sharding import Mesh
from jax.sharding import PartitionSpec as P

BF = jnp.bfloat16
F32 = jnp.float32
ROWS = 256
VMEM_BYTES = 14 * 2**20


def dot(a, b, ca, cb):
    return lax.dot_general(a, b, (((ca,), (cb,)), ((), ())), preferred_element_type=F32)


def activate(gate_pre, up_pre, down_grad):
    sigmoid_val = jax.nn.sigmoid(gate_pre)
    swish_val = gate_pre * sigmoid_val
    hidden = (swish_val * up_pre).astype(BF)
    slope_val = sigmoid_val * (1.0 + gate_pre * (1.0 - sigmoid_val))
    gate_grad = (down_grad * up_pre * slope_val).astype(BF)
    up_grad = (down_grad * swish_val).astype(BF)
    return hidden, gate_grad, up_grad


def call(body, outs, flops, args):
    spaces = [pltpu.SMEM if a.ndim == 1 else pltpu.VMEM for a in args]
    in_specs = [pl.BlockSpec(memory_space=space) for space in spaces]
    moved = sum(a.size * a.dtype.itemsize for a in (*args, *outs))
    return pl.pallas_call(
        body,
        out_shape=outs,
        in_specs=in_specs,
        out_specs=[pl.BlockSpec(memory_space=pltpu.VMEM) for _ in outs],
        compiler_params=pltpu.CompilerParams(vmem_limit_bytes=VMEM_BYTES),
        cost_estimate=pl.CostEstimate(flops=flops, bytes_accessed=moved, transcendentals=0),
    )(*args)


def by_expert(rows, routed):
    return [jnp.where(m, rows, jnp.zeros_like(rows)) for m in (routed > 0.0, routed < 0.0)]


def forward_body(side, at_ref, expert_ref, got_ref, wg_ref, wu_ref, wd_ref, keep_ref, *give_refs):
    n_yh, part, width = keep_ref.shape
    experts = wg_ref.shape[0]
    _, _, own, cols = got_ref.shape
    hid = width // 3
    parity, core = lax.rem(at_ref[0] + side, 2), at_ref[1]
    per = 2 * part
    owners = per // own
    group = ROWS // per

    @pl.loop(0, n_yh // group)
    def _(i):
        starts = [2 * (i * group + q) + parity for q in range(group)]
        expert = jnp.concatenate(
            [expert_ref[pl.ds(pl.multiple_of(s * per, per), per), :] for s in starts]
        )
        masked = []
        for kind in range(2):
            rows = [got_ref[pl.ds(s * owners, owners), kind].reshape(per, cols) for s in starts]
            rows = jnp.concatenate(rows)
            if kind:
                rows = (rows.astype(F32) * jnp.abs(expert)).astype(BF)
            masked.append(by_expert(rows, expert))
        for k, w_ref in enumerate((wg_ref, wu_ref, wd_ref)):
            out = 0.0
            for e in range(experts):
                out = out + dot(masked[k // 2][e], w_ref[e], 1, k // 2)
            to = slice(k * hid, (k + 1) * hid)
            for q in range(group):
                even = out[q * per : q * per + part]
                odd = out[q * per + part : (q + 1) * per]
                keep_ref[i * group + q, :, to] = jnp.where(core == 0, even, odd)
                give = jnp.where(core == 0, odd, even).astype(BF)
                if len(give_refs) == 1:
                    give_refs[0][i * group + q, :, to] = give
                else:
                    give_refs[k][i * group + q] = give


def terms_body(side, at_ref, expert_ref, gate_ref, up_ref, mine_ref, other_ref, *refs):
    out_ref = refs[-1]
    n_yh, part, width = mine_ref.shape
    experts, _, hid = gate_ref.shape
    parity, core = lax.rem(at_ref[0] + side, 2), at_ref[1]
    per = 2 * part
    group = ROWS // per

    @pl.loop(0, n_yh // group)
    def _(i):
        expert, rows = [], []
        for q in range(group):
            start = (2 * (i * group + q) + parity) * per
            expert.append(expert_ref[pl.ds(pl.multiple_of(start, per), per), :])
            mine, other = mine_ref[i * group + q], other_ref[i * group + q]
            rows += [jnp.where(core == 0, mine, other), jnp.where(core == 0, other, mine)]
        expert, rows = jnp.concatenate(expert), jnp.concatenate(rows)
        gates = by_expert(rows[:, :hid], expert)
        ups = by_expert(rows[:, hid:], expert)
        out = 0.0
        for e in range(experts):
            out = out + dot(gates[e], gate_ref[e], 1, 1) + dot(ups[e], up_ref[e], 1, 1)
        out = out.astype(BF)
        for q in range(group):
            piece = out[q * per : (q + 1) * per]
            if side:
                out_ref[i * group + q, parity] = piece
                out_ref[i * group + q, 1 - parity] = refs[0][i * group + q]
            else:
                out_ref[i * group + q] = piece


def order_body(at_ref, mine_ref, other_ref, far_mine_ref, far_other_ref, out_ref):
    parity, core = at_ref[0], at_ref[1]

    @pl.loop(0, mine_ref.shape[0])
    def _(i):
        out_ref[i, parity, core] = mine_ref[i]
        out_ref[i, parity, 1 - core] = other_ref[i]
        out_ref[i, 1 - parity, core] = far_mine_ref[i]
        out_ref[i, 1 - parity, 1 - core] = far_other_ref[i]


def total_body(x_ref, out_ref):
    out = x_ref[0].astype(F32)
    for i in range(1, x_ref.shape[0]):
        out = out + x_ref[i].astype(F32)
    out_ref[...] = out.astype(BF)


def make(n_yh, n_yl, n_core, n_x, n_z):
    along_y, dp, cuts = ("yh", "yl"), ("yh", "yl", "core"), ("x", "z")
    n_y = n_yh * n_yl
    n_dp, n_cuts = n_y * n_core, n_x * n_z
    swap = [(i, n_core - 1 - i) for i in range(n_core)]
    left = [(i, i ^ 1) for i in range(n_y)]
    right = [(i, (i + 1) % n_y if i % 2 else (i - 1) % n_y) for i in range(n_y)]

    def per_device(tokens, cotangent, w_gate, w_up, w_down, row_token, block_expert, gate_weight):
        own, cols = tokens.shape
        n_tok = row_token.shape[0]
        experts, _, hid = w_gate.shape
        blk = n_tok // block_expert.shape[0]
        part = n_tok // n_dp
        at = jnp.stack([lax.axis_index("yl"), lax.axis_index("core")]).astype(jnp.int32)
        work = 2 * n_tok * experts * cols * hid

        def exchange(v, axes):
            return lax.all_to_all(v, axes, split_axis=0, concat_axis=0, tiled=True)

        def spread(v, n):
            return jnp.broadcast_to(v[None], (n,) + v.shape)

        def halves(v):
            half = v.shape[-1] // 2
            return v[..., :half], v[..., half:]

        def neighbours(v):
            return lax.ppermute(v[0], along_y, left), lax.ppermute(v[1], along_y, right)

        got = exchange(spread(jnp.stack([tokens, cotangent]), n_z), "z")
        expert_row = jnp.repeat(block_expert[:, 0], blk)
        routed_row = jnp.where(expert_row == 0, gate_weight, -gate_weight)
        holds = row_token[None, :] == jnp.arange(n_tok, dtype=jnp.int32)[:, None]
        routed = jnp.sum(jnp.where(holds, routed_row[None, :], 0.0), axis=1)[:, None]
        got = exchange(spread(got.reshape(n_z, 2, own, cols), n_x), "x")
        got = got.reshape(n_cuts, 2, own, cols)

        def forward(side, pieces):
            width = 3 * hid // pieces
            outs = [jax.ShapeDtypeStruct((n_yh, part, 3 * hid), F32)]
            outs += [jax.ShapeDtypeStruct((n_yh, part, width), BF)] * pieces
            args = (at, routed, got, w_gate, w_up, w_down)
            body = functools.partial(forward_body, side)
            return call(body, outs, 3 * work // 2, args)

        far_keep, far_give = forward(1, 1)
        far_came = lax.ppermute(far_give, "core", swap)
        keep, *give = forward(0, 3)
        far = halves((far_keep + far_came.astype(F32)).astype(BF))
        far, give = lax.optimization_barrier((far, give))
        near = neighbours(far)
        came = jnp.concatenate([lax.ppermute(g, "core", swap) for g in give], axis=-1)
        chips = keep + came.astype(F32) + jnp.concatenate(near, axis=-1).astype(F32)
        chips = chips.astype(BF)
        pre = jnp.sum(exchange(chips, "yh").astype(F32), axis=0)
        hidden, gate_grad, up_grad = activate(
            pre[:, :hid], pre[:, hid : 2 * hid], pre[:, 2 * hid :]
        )
        hidden = lax.all_gather(hidden, dp, axis=0, tiled=True)
        grads = exchange(spread(jnp.concatenate([gate_grad, up_grad], axis=1), n_yh), "yh")
        grads = grads.reshape(n_yh, part, 2 * hid)
        near = neighbours(halves(grads))
        other = lax.ppermute(grads, "core", swap)
        outs = [jax.ShapeDtypeStruct((n_yh, n_core * part, cols), BF)]
        args = (at, routed, w_gate, w_up, grads, other)
        (own_terms,) = call(functools.partial(terms_body, 0), outs, work, args)
        far = jnp.concatenate(near, axis=-1)
        far_other = lax.ppermute(far, "core", swap)
        outs = [jax.ShapeDtypeStruct((n_yh, n_yl, n_core * part, cols), BF)]
        args = (at, routed, w_gate, w_up, far, far_other, own_terms)
        (terms,) = call(functools.partial(terms_body, 1), outs, work, args)
        terms = exchange(terms.reshape(n_cuts, own, cols), cuts)
        outs = [jax.ShapeDtypeStruct((own, cols), BF)]
        (token_grad,) = call(total_body, outs, terms.size, (terms,))

        outs = [jax.ShapeDtypeStruct((n_yh, n_yl, n_core, part, 2 * hid), BF)]
        (grads,) = call(order_body, outs, grads.size, (at, grads, other, far, far_other))
        grads = grads.reshape(n_tok, 2 * hid)
        tok, cot = got[:, 0].reshape(n_tok, cols), got[:, 1].reshape(n_tok, cols)
        cot = (cot.astype(F32) * jnp.abs(routed)).astype(BF)
        masks = [routed > 0.0, routed < 0.0]
        tok_by = jnp.concatenate([jnp.where(m, tok, 0) for m in masks], axis=1)
        grad_gate = dot(tok_by, grads[:, :hid], 0, 0).astype(BF).reshape(w_gate.shape)
        grads, hidden = lax.optimization_barrier((grads, hidden))
        grad_up = dot(tok_by, grads[:, hid:], 0, 0).astype(BF).reshape(w_up.shape)
        grad_down = [dot(hidden, jnp.where(m, cot, 0), 0, 0).astype(BF) for m in masks]
        return token_grad, grad_gate, grad_up, jnp.stack(grad_down)

    return per_device


def solution(mesh):
    sizes, axes = (4, 2, 2, 4, 8), ("yh", "yl", "core", "x", "z")
    fine = Mesh(mesh.devices.reshape(sizes), axes)
    dp, cuts = ("yh", "yl", "core"), ("x", "z")
    return jax.shard_map(
        make(*sizes),
        mesh=fine,
        in_specs=(
            P(cuts, dp),
            P(cuts, dp),
            P(None, dp, cuts),
            P(None, dp, cuts),
            P(None, cuts, dp),
            P(),
            P(),
            P(),
        ),
        out_specs=(P(cuts, dp), P(None, dp, cuts), P(None, dp, cuts), P(None, cuts, dp)),
        check_vma=False,
    )
```

```python
import functools

import jax
import jax.numpy as jnp
from jax import lax
from jax.experimental import pallas as pl
from jax.experimental.pallas import tpu as pltpu
from jax.sharding import Mesh
from jax.sharding import PartitionSpec as P

BF = jnp.bfloat16
F32 = jnp.float32
ROWS = 256
VMEM_BYTES = 14 * 2**20


def dot(a, b, ca, cb):
    return lax.dot_general(a, b, (((ca,), (cb,)), ((), ())), preferred_element_type=F32)


def activate(gate_pre, up_pre, down_grad):
    sigmoid_val = jax.nn.sigmoid(gate_pre)
    swish_val = gate_pre * sigmoid_val
    hidden = (swish_val * up_pre).astype(BF)
    slope_val = sigmoid_val * (1.0 + gate_pre * (1.0 - sigmoid_val))
    gate_grad = (down_grad * up_pre * slope_val).astype(BF)
    up_grad = (down_grad * swish_val).astype(BF)
    return hidden, gate_grad, up_grad


def call(body, outs, flops, args):
    spaces = [pltpu.SMEM if a.ndim == 1 else pltpu.VMEM for a in args]
    in_specs = [pl.BlockSpec(memory_space=space) for space in spaces]
    moved = sum(a.size * a.dtype.itemsize for a in (*args, *outs))
    return pl.pallas_call(
        body,
        out_shape=outs,
        in_specs=in_specs,
        out_specs=[pl.BlockSpec(memory_space=pltpu.VMEM) for _ in outs],
        compiler_params=pltpu.CompilerParams(vmem_limit_bytes=VMEM_BYTES),
        cost_estimate=pl.CostEstimate(flops=flops, bytes_accessed=moved, transcendentals=0),
    )(*args)


def by_expert(rows, routed):
    return [jnp.where(m, rows, jnp.zeros_like(rows)) for m in (routed > 0.0, routed < 0.0)]


def forward_body(side, at_ref, expert_ref, got_ref, wg_ref, wu_ref, wd_ref, keep_ref, *give_refs):
    n_yh, part, width = keep_ref.shape
    experts = wg_ref.shape[0]
    _, _, own, cols = got_ref.shape
    hid = width // 3
    parity, core = lax.rem(at_ref[0] + side, 2), at_ref[1]
    per = 2 * part
    owners = per // own
    group = ROWS // per

    @pl.loop(0, n_yh // group)
    def _(i):
        starts = [2 * (i * group + q) + parity for q in range(group)]
        expert = jnp.concatenate(
            [expert_ref[pl.ds(pl.multiple_of(s * per, per), per), :] for s in starts]
        )
        masked = []
        for kind in range(2):
            rows = [got_ref[pl.ds(s * owners, owners), kind].reshape(per, cols) for s in starts]
            rows = jnp.concatenate(rows)
            if kind:
                rows = (rows.astype(F32) * jnp.abs(expert)).astype(BF)
            masked.append(by_expert(rows, expert))
        for k, w_ref in enumerate((wg_ref, wu_ref, wd_ref)):
            out = 0.0
            for e in range(experts):
                out = out + dot(masked[k // 2][e], w_ref[e], 1, k // 2)
            to = slice(k * hid, (k + 1) * hid)
            for q in range(group):
                even = out[q * per : q * per + part]
                odd = out[q * per + part : (q + 1) * per]
                keep_ref[i * group + q, :, to] = jnp.where(core == 0, even, odd)
                give = jnp.where(core == 0, odd, even).astype(BF)
                if len(give_refs) == 1:
                    give_refs[0][i * group + q, :, to] = give
                else:
                    give_refs[k][i * group + q] = give


def terms_body(side, at_ref, expert_ref, gate_ref, up_ref, mine_ref, other_ref, *refs):
    out_ref = refs[-1]
    n_yh, part, width = mine_ref.shape
    experts, _, hid = gate_ref.shape
    parity, core = lax.rem(at_ref[0] + side, 2), at_ref[1]
    per = 2 * part
    group = ROWS // per

    @pl.loop(0, n_yh // group)
    def _(i):
        expert, rows = [], []
        for q in range(group):
            start = (2 * (i * group + q) + parity) * per
            expert.append(expert_ref[pl.ds(pl.multiple_of(start, per), per), :])
            mine, other = mine_ref[i * group + q], other_ref[i * group + q]
            rows += [jnp.where(core == 0, mine, other), jnp.where(core == 0, other, mine)]
        expert, rows = jnp.concatenate(expert), jnp.concatenate(rows)
        gates = by_expert(rows[:, :hid], expert)
        ups = by_expert(rows[:, hid:], expert)
        out = 0.0
        for e in range(experts):
            out = out + dot(gates[e], gate_ref[e], 1, 1) + dot(ups[e], up_ref[e], 1, 1)
        out = out.astype(BF)
        for q in range(group):
            piece = out[q * per : (q + 1) * per]
            if side:
                out_ref[i * group + q, parity] = piece
                out_ref[i * group + q, 1 - parity] = refs[0][i * group + q]
            else:
                out_ref[i * group + q] = piece


def order_body(at_ref, mine_ref, other_ref, far_mine_ref, far_other_ref, out_ref):
    parity, core = at_ref[0], at_ref[1]

    @pl.loop(0, mine_ref.shape[0])
    def _(i):
        out_ref[i, parity, core] = mine_ref[i]
        out_ref[i, parity, 1 - core] = other_ref[i]
        out_ref[i, 1 - parity, core] = far_mine_ref[i]
        out_ref[i, 1 - parity, 1 - core] = far_other_ref[i]


def total_body(x_ref, out_ref):
    out = x_ref[0].astype(F32)
    for i in range(1, x_ref.shape[0]):
        out = out + x_ref[i].astype(F32)
    out_ref[...] = out.astype(BF)


def make(n_yh, n_yl, n_core, n_x, n_z):
    along_y, dp, cuts = ("yh", "yl"), ("yh", "yl", "core"), ("x", "z")
    n_y = n_yh * n_yl
    n_dp, n_cuts = n_y * n_core, n_x * n_z
    swap = [(i, n_core - 1 - i) for i in range(n_core)]
    left = [(i, i ^ 1) for i in range(n_y)]
    right = [(i, (i + 1) % n_y if i % 2 else (i - 1) % n_y) for i in range(n_y)]

    def per_device(tokens, cotangent, w_gate, w_up, w_down, row_token, block_expert, gate_weight):
        own, cols = tokens.shape
        n_tok = row_token.shape[0]
        experts, _, hid = w_gate.shape
        blk = n_tok // block_expert.shape[0]
        part = n_tok // n_dp
        at = jnp.stack([lax.axis_index("yl"), lax.axis_index("core")]).astype(jnp.int32)
        work = 2 * n_tok * experts * cols * hid

        def exchange(v, axes):
            return lax.all_to_all(v, axes, split_axis=0, concat_axis=0, tiled=True)

        def spread(v, n):
            return jnp.broadcast_to(v[None], (n,) + v.shape)

        def halves(v):
            half = v.shape[-1] // 2
            return v[..., :half], v[..., half:]

        def neighbours(v):
            return lax.ppermute(v[0], along_y, left), lax.ppermute(v[1], along_y, right)

        got = exchange(spread(jnp.stack([tokens, cotangent]), n_z), "z")
        expert_row = jnp.repeat(block_expert[:, 0], blk)
        routed_row = jnp.where(expert_row == 0, gate_weight, -gate_weight)
        holds = row_token[None, :] == jnp.arange(n_tok, dtype=jnp.int32)[:, None]
        routed = jnp.sum(jnp.where(holds, routed_row[None, :], 0.0), axis=1)[:, None]
        got = exchange(spread(got.reshape(n_z, 2, own, cols), n_x), "x")
        got = got.reshape(n_cuts, 2, own, cols)

        def forward(side, pieces):
            width = 3 * hid // pieces
            outs = [jax.ShapeDtypeStruct((n_yh, part, 3 * hid), F32)]
            outs += [jax.ShapeDtypeStruct((n_yh, part, width), BF)] * pieces
            args = (at, routed, got, w_gate, w_up, w_down)
            body = functools.partial(forward_body, side)
            return call(body, outs, 3 * work // 2, args)

        far_keep, far_give = forward(1, 1)
        far_came = lax.ppermute(far_give, "core", swap)
        keep, *give = forward(0, 3)
        far = halves((far_keep + far_came.astype(F32)).astype(BF))
        far, give = lax.optimization_barrier((far, give))
        near = neighbours(far)
        came = jnp.concatenate([lax.ppermute(g, "core", swap) for g in give], axis=-1)
        chips = keep + came.astype(F32) + jnp.concatenate(near, axis=-1).astype(F32)
        chips = chips.astype(BF)
        pre = jnp.sum(exchange(chips, "yh").astype(F32), axis=0)
        hidden, gate_grad, up_grad = activate(
            pre[:, :hid], pre[:, hid : 2 * hid], pre[:, 2 * hid :]
        )
        hidden = lax.all_gather(hidden, dp, axis=0, tiled=True)
        grads = exchange(spread(jnp.concatenate([gate_grad, up_grad], axis=1), n_yh), "yh")
        grads = grads.reshape(n_yh, part, 2 * hid)
        near = neighbours(halves(grads))
        other = lax.ppermute(grads, "core", swap)
        outs = [jax.ShapeDtypeStruct((n_yh, n_core * part, cols), BF)]
        args = (at, routed, w_gate, w_up, grads, other)
        (own_terms,) = call(functools.partial(terms_body, 0), outs, work, args)
        far = jnp.concatenate(near, axis=-1)
        far_other = lax.ppermute(far, "core", swap)
        outs = [jax.ShapeDtypeStruct((n_yh, n_yl, n_core * part, cols), BF)]
        args = (at, routed, w_gate, w_up, far, far_other, own_terms)
        (terms,) = call(functools.partial(terms_body, 1), outs, work, args)
        terms = exchange(terms.reshape(n_cuts, own, cols), cuts)
        outs = [jax.ShapeDtypeStruct((own, cols), BF)]
        (token_grad,) = call(total_body, outs, terms.size, (terms,))

        outs = [jax.ShapeDtypeStruct((n_yh, n_yl, n_core, part, 2 * hid), BF)]
        (grads,) = call(order_body, outs, grads.size, (at, grads, other, far, far_other))
        grads, routed = lax.optimization_barrier((grads.reshape(n_tok, 2 * hid), routed))
        tok, cot = got[:, 0].reshape(n_tok, cols), got[:, 1].reshape(n_tok, cols)
        cot = (cot.astype(F32) * jnp.abs(routed)).astype(BF)
        masks = [routed > 0.0, routed < 0.0]
        tok_by = jnp.concatenate([jnp.where(m, tok, 0) for m in masks], axis=1)
        grad_gate = dot(tok_by, grads[:, :hid], 0, 0).astype(BF).reshape(w_gate.shape)
        grads, hidden = lax.optimization_barrier((grads, hidden))
        grad_up = dot(tok_by, grads[:, hid:], 0, 0).astype(BF).reshape(w_up.shape)
        grad_down = [dot(hidden, jnp.where(m, cot, 0), 0, 0).astype(BF) for m in masks]
        return token_grad, grad_gate, grad_up, jnp.stack(grad_down)

    return per_device


def solution(mesh):
    sizes, axes = (4, 2, 2, 4, 8), ("yh", "yl", "core", "x", "z")
    fine = Mesh(mesh.devices.reshape(sizes), axes)
    dp, cuts = ("yh", "yl", "core"), ("x", "z")
    return jax.shard_map(
        make(*sizes),
        mesh=fine,
        in_specs=(
            P(cuts, dp),
            P(cuts, dp),
            P(None, dp, cuts),
            P(None, dp, cuts),
            P(None, cuts, dp),
            P(),
            P(),
            P(),
        ),
        out_specs=(P(cuts, dp), P(None, dp, cuts), P(None, dp, cuts), P(None, cuts, dp)),
        check_vma=False,
    )
```
